128 devices in a mesh: surf: 32 (over x, y, core), dir: 4 (over z).
Axes of the slice: x: 4, y: 4, z: 4, core: 2. Of those that a mesh axis runs over, the one named last changes fastest.
Arguments:
- densities: float32 [512, 32768], P(None, ('surf', 'dir')), may hold values from -6 to 6
- weights: float32 [32768], P(('surf', 'dir')), may hold values from 0.1 to 1
- coords: float32 [3, 32768], P(None, ('surf', 'dir')), may hold values from -1 to 1
- counts: int32 [128], P(('surf', 'dir')), may hold values from 0 to 256, as said below
- wave: float32 [3, 4, 8192], P(None, 'dir'), may hold values from -20 to 20
Outputs:
- pattern: float32 [512, 4, 8192], P(None, 'dir', 'surf')
The draws below stay inside these ranges and needn't reach their ends.
Inputs may be any that keep to these rules, and one draw needn't show every extreme that they name: The counts sum to 16384. For every device q, the counts of the devices before q sum to between q * 128 and (q + 1) * 128. One count equals 256 and one equals 0.
All inputs are finite; a program needn't handle non-finite values.
Results may differ from the reference program's by a relative error of at most 0.0037.
Values sent between devices are 32-bit elements; how exact they have to be, the bound alone decides.
A program may use at most 128 MiB of HBM per device.

```python
import math
import jax
import jax.numpy as jnp
from jax import lax

PB_DEV = 128
R = 256
DIRS = 32768
CAP = 256
NPTS = 16384
DPD = 8192
N_DIR = 4
DEVICES = 128


def draw_counts(key, part):
    key = jax.random.fold_in(key, 11)
    initial_key, second_key = jax.random.split(key)
    spots = jnp.arange(DEVICES, dtype=jnp.int32)
    running_tally = jax.random.randint(initial_key, (DEVICES,), 0, PB_DEV + 1).astype(jnp.int32)
    chosen = jax.random.randint(second_key, (), 0, DEVICES - 2).astype(jnp.int32)
    running_tally = jnp.where(spots == chosen, PB_DEV, running_tally)
    running_tally = jnp.where((spots == chosen - 1) | (spots == chosen + 1) | (spots == DEVICES - 1), 0, running_tally).astype(jnp.int32)
    prior_neighbour = jnp.concatenate([jnp.zeros((1,), jnp.int32), running_tally[:-1]])
    return (PB_DEV + running_tally - prior_neighbour).astype(jnp.int32)


def shard_levels(own_key, extent, pieces, smallest, high):
    factor_of = 1.0
    for dim, shards_of in pieces:
        heights = jax.random.uniform(jax.random.fold_in(jax.random.fold_in(own_key, 6), dim), (shards_of,), jnp.float32, smallest / len(pieces), high / len(pieces))
        factor_of = factor_of * jnp.repeat(jnp.exp(heights), extent[dim] // shards_of).reshape((-1,) + (1,) * (len(extent) - 1 - dim))
    return factor_of


def noise(rng, extent, deviation, limit, shards=(), held_as=jnp.bfloat16):
    drawn = jax.random.normal(rng, extent, jnp.float32) * deviation
    if len(shards) > 0:
        drawn = shard_levels(rng, extent, shards, -0.22, 0.18) * drawn
    return jnp.clip(drawn, min=-limit, max=limit).astype(held_as)


def setup_inputs(seed: int = 0) -> dict:
    key_of = jax.random.split(jax.random.key(seed), 6)
    return {
        "densities": noise(key_of[0], (2 * R, DEVICES * CAP), 1.0, 6.0, ((1, 128),), jnp.float32),
        "weights": jnp.clip(jnp.exp(math.log(1.0) - 2.3025851 * jax.random.uniform(key_of[1], (DEVICES * CAP,), jnp.float32) ** shard_levels(key_of[1], (DEVICES * CAP,), ((0, 128),), -0.2, 0.2)), 0.1, 1.0),
        "coords": jnp.clip(jax.random.uniform(key_of[2], (3, DEVICES * CAP), jnp.float32, -1.0, 1.0) * shard_levels(key_of[2], (3, DEVICES * CAP), ((1, 128),), -0.4, 0.0), -1.0, 1.0),
        "counts": draw_counts(jax.random.fold_in(key_of[5], 71), 0),
        "wave": jnp.clip(jax.random.uniform(key_of[4], (3, N_DIR, DPD), jnp.float32, -20.0, 20.0) * shard_levels(key_of[4], (3, N_DIR, DPD), ((1, 4),), -0.4, 0.0), -20.0, 20.0),
    }


def block_terms(strength, xyz, kvec):
    phase = xyz[0][:, None] * kvec[0][None, :] + xyz[1][:, None] * kvec[1][None, :] + xyz[2][:, None] * kvec[2][None, :]
    cosine = lax.optimization_barrier(jnp.cos(phase).astype(jnp.bfloat16)).astype(jnp.float32)
    sine = lax.optimization_barrier(jnp.sin(phase).astype(jnp.bfloat16)).astype(jnp.float32)
    first = jnp.dot(strength, cosine, precision=lax.Precision.HIGHEST)
    second = jnp.dot(strength, sine, precision=lax.Precision.HIGHEST)
    half = strength.shape[0] // 2
    return jnp.concatenate([first[:half] + second[half:], first[half:] - second[:half]], axis=0)

def reference(densities, weights, coords, counts, wave):
    slots = weights.shape[0] // counts.shape[0]
    ends = jnp.cumsum(counts).astype(jnp.int32)
    starts = (ends - counts).astype(jnp.int32)
    points = jnp.arange(NPTS, dtype=jnp.int32)
    owner = jnp.searchsorted(ends, points, side='right').astype(jnp.int32)
    column = (owner * slots + points - starts[owner]).astype(jnp.int32)
    scale_factor = 1.0 / math.sqrt(NPTS)
    rounded = lax.optimization_barrier((weights[None, :] * densities * scale_factor).astype(jnp.bfloat16))
    strength = rounded.astype(jnp.float32)[:, column]
    xyz = coords[:, column]
    width = math.gcd(DIRS, 1024)
    kvec = wave.reshape(3, DIRS // width, width).transpose(1, 0, 2)
    block_groups = lax.map(lambda kk: block_terms(strength, xyz, kk), kvec)
    whole = block_groups.transpose(1, 0, 2).reshape(2 * R, DIRS)
    return whole.reshape(2 * R, N_DIR, DIRS // N_DIR)
```

```python
import functools
import math

import numpy as np

import jax
import jax.numpy as jnp
from jax import lax
from jax.experimental import pallas as pl
from jax.experimental.pallas import tpu as pltpu
from jax.sharding import PartitionSpec as P

MESH = pl.DeviceIdType.MESH
F32, BF16, I32 = jnp.float32, jnp.bfloat16, jnp.int32
N = 4
PTS = 128
NCH = 4
HB = 64
NDIR = 2048
BLK = 256


def _fit(f, terms, odd):
    x = np.cos(np.linspace(0, np.pi / 2, 2001)) * 0.5
    a = np.stack([x ** (2 * k + odd) for k in range(terms)], 1)
    w = np.ones_like(x)
    for _ in range(60):
        c = np.linalg.lstsq(a * w[:, None], f(x) * w, rcond=None)[0]
        e = np.abs(a @ c - f(x))
        w = w * np.sqrt(e / e.max() + 0.02)
        w = w / w.max()
    return [float(np.float32(v)) for v in c * math.sqrt(2.0)]


SIN = _fit(lambda r: np.sin(np.pi * r), 3, 1)
COS = _fit(lambda r: np.cos(np.pi * r), 4, 0)


def horner(q, c):
    acc = c[-1] * q + c[-2]
    for k in c[-3::-1]:
        acc = acc * q + k
    return acc


def split3(v):
    a = v.astype(BF16).astype(F32)
    b = (v - a).astype(BF16).astype(F32)
    return a, b, (v - a) - b


E_STEPS = {
    0: [(1, 0)], 1: [(0, 1)], 2: [(2, 0)], 3: [(0, 2)], 4: [(1, 1)], 5: [(3, 0)], 6: [(1, 2)], 7: [(0, 3)],
    8: [(2, 1)], 9: [(2, 2)], 10: [(1, 3)], 11: [(3, 1)], 12: [(0, 4)], 13: [(3, 2)], 14: [(2, 3)], 15: [],
}
M_STEPS = {1: [(1, 4)], 2: [(3, 3)], 6: [(2, 4)], 10: [(3, 4)]}


def kernel(
    dens, wts, coords, counts, wave, out,
    cnt1, cnt2, crd, cin, cout, kf, kmat, keep, sout, sin_, G, E, L, Pm, Po, Cx, Hp, Hm, Rp, Rm,
    s1s, s1r, s2s, s2r, scs, scr, sgs, sgr, shs, shr, ggs, ggr, cxs, cxr, hs, hr, rs, rr,
):
    surf, z = lax.axis_index("surf"), lax.axis_index("dir")
    x, y, c = surf // 8, (surf // 2) % N, surf % 2
    q = surf * N + z

    def dev(xx, yy, cc, zz):
        return ((xx * N + yy) * 2 + cc, zz)

    def up(v, k):
        return lax.rem(v + (k + N), N)

    def remote(src, dst, ss, rs_, to):
        return pltpu.make_async_remote_copy(
            src_ref=src, dst_ref=dst, send_sem=ss, recv_sem=rs_, device_id=to, device_id_type=MESH
        )

    me8 = c * N + z
    peers8 = []
    for k in range(1, 8):
        o = lax.rem(me8 + k, 8)
        peers8.append(dev(x, y, o // N, lax.rem(o, N)))
    peers16 = [dev(up(x, i), up(y, j), c, z) for i in range(N) for j in range(N) if i or j]
    peersyz = [(i, j) for i in range(N) for j in range(N) if i or j]
    qn, qp = lax.rem(q + 1, 128), lax.rem(q + 127, 128)
    nxt, prv = (qn // N, lax.rem(qn, N)), (qp // N, lax.rem(qp, N))

    barrier = pltpu.get_barrier_semaphore()
    extra = [dev(x, up(y, i), c, up(z, j)) for i, j in peersyz if i and j]
    greet = peers8 + peers16 + extra + [nxt, prv]
    for to in greet:
        pl.semaphore_signal(barrier, inc=1, device_id=to, device_id_type=MESH)

    kf[...] = jnp.zeros_like(kf)
    for t, dx in enumerate((2, 1, 3, 0)):
        for h in range(2):
            cc = c if h == 0 else 1 - c
            at = pl.multiple_of((up(x, dx) * 8 + y * 2 + cc) * BLK, BLK)
            for k in range(3):
                kf[k : k + 1, t * 512 + h * BLK : t * 512 + (h + 1) * BLK] = (
                    wave[k, :, pl.ds(at, BLK)] * (1.0 / (2.0 * math.pi))
                )
    k1, k2, k3 = split3(kf[...])
    kmat[...] = jnp.concatenate([k1, k2, k1, k3, k2, k1, jnp.zeros((80, NDIR), F32)], 0).astype(BF16)
    cin[...] = jnp.zeros_like(cin)
    cin[0:3, :] = coords[...]
    cnt = counts[0]
    cnt1[me8] = jnp.full((8, 128), cnt, I32)

    pl.semaphore_wait(barrier, len(greet))

    n1 = [
        remote(cnt1.at[me8], cnt1.at[me8], s1s.at[k], s1r.at[k], peers8[k]) for k in range(7)
    ]
    for d in n1:
        d.start()
    for d in n1:
        d.wait_recv()
    total8 = jnp.zeros((8, 128), I32)
    before = jnp.zeros((8, 128), I32)
    for k in range(8):
        v = cnt1[k]
        total8 = total8 + v
        before = before + v * jnp.where(k < me8, 1, 0)
    me16 = x * N + y
    cnt2[me16] = total8
    n2 = [
        remote(cnt2.at[me16], cnt2.at[me16], s2s.at[k], s2r.at[k], peers16[k]) for k in range(15)
    ]
    for d in n2:
        d.start()
    for d in n2:
        d.wait_recv()
    for k in range(16):
        before = before + cnt2[k] * jnp.where(k < me16, 1, 0)
    shift = before - q * PTS

    srow = jnp.broadcast_to(shift[0:1, :], (256, 128))
    srow = jnp.concatenate([srow, srow], 1)
    slot = lax.broadcasted_iota(I32, (256, 256), 0)
    col = lax.broadcasted_iota(I32, (256, 256), 1)
    pick = jnp.where((col - slot == srow) & (slot < cnt), 1.0, 0.0).astype(BF16)

    ca, cb, cc_ = split3(cin[...])
    cp = jnp.dot(jnp.concatenate([ca, cb, cc_], 0).astype(BF16), pick, preferred_element_type=F32)
    packed = cp[0:8] + cp[8:16] + cp[16:24]
    cout[...] = packed[:, 128:]
    dc = remote(cout, crd.at[16], scs.at[0], scr.at[0], nxt)
    dc.start()

    scale = 1.0 / math.sqrt(PTS * 128)
    w = wts[...]
    dsh = []
    for ch in range(NCH):
        ra, rb = slice(ch * HB, (ch + 1) * HB), slice(256 + ch * HB, 256 + (ch + 1) * HB)
        v = jnp.concatenate([dens[ra, :], dens[rb, :]], 0)
        v = ((w * v) * scale).astype(BF16)
        moved = jnp.dot(v, pick, preferred_element_type=F32)
        keep[ch] = moved[:, :128]
        sout[ch] = moved[:, 128:]
        d = remote(sout.at[ch], sin_.at[ch], shs.at[ch], shr.at[ch], nxt)
        d.start()
        dsh.append(d)

    own = y * N + z
    dc.wait_recv()
    crd[own] = packed[:, :128] + crd[16]
    dg = [
        remote(crd.at[own], crd.at[own], sgs.at[k], sgr.at[k], dev(x, up(y, i), c, up(z, j)))
        for k, (i, j) in enumerate(peersyz)
    ]
    for d in dg:
        d.start()

    def gcopies(ch, st):
        sem = lambda n: (ggs.at[ch, st * 4 + n], ggr.at[ch, st * 4 + n])
        yn, yp, zn, zp = (dev(x, up(y, 1), c, z), dev(x, up(y, -1), c, z), dev(x, y, c, up(z, 1)), dev(x, y, c, up(z, -1)))
        ym, yq, zm, zq = up(y, -1), up(y, 1), up(z, -1), up(z, 1)
        lo, lo1, lo2 = pl.ds(0, 64), pl.ds(0, 32), pl.ds(32, 32)
        hi, hi1, hi2 = pl.ds(64, 64), pl.ds(64, 32), pl.ds(96, 32)
        al = pl.ds(0, N)
        if st == 0:
            parts = [((y, z, lo), yn), ((y, z, lo), yp), ((y, z, hi), zn), ((y, z, hi), zp)]
        elif st == 1:
            parts = [((ym, z, lo1), yn), ((yq, z, lo2), yp), ((y, zm, hi1), zn), ((y, zq, hi2), zp)]
        elif st == 2:
            parts = [((al, z, lo), zn), ((al, z, lo), zp), ((y, al, hi), yn), ((y, al, hi), yp)]
        else:
            parts = [((al, zm, lo1), zn), ((al, zq, lo2), zp), ((ym, al, hi1), yn), ((yq, al, hi2), yp)]
        return [remote(G.at[(ch,) + p], G.at[(ch,) + p], *sem(n), to) for n, (p, to) in enumerate(parts)]

    def gstep(ch, st):
        if st == 0:
            dsh[ch].wait_recv()
            G[ch, y, z] = keep[ch] + sin_[ch]
        else:
            for d in gcopies(ch, st - 1):
                d.wait_recv()
        if st < 4:
            for d in gcopies(ch, st):
                d.start()

    gstep(0, 0)

    @pl.loop(0, 16)
    def _(it):
        @pl.when(it == 1)
        def _():
            for d in dg:
                d.wait_recv()

        b = lax.rem(own + it, 16)
        a1, a2, a3 = split3(crd[b])
        xt = jnp.concatenate([a1, a1, a2, a1, a2, a3, jnp.zeros((80, 128), F32)], 0)
        xm = xt.T.astype(BF16)
        rows = pl.multiple_of(b * PTS, PTS)
        for j in range(NDIR // 256):
            cols = slice(j * 256, (j + 1) * 256)
            turn = jnp.dot(xm, kmat[:, cols], preferred_element_type=F32)
            r = turn - jnp.round(turn)
            r2 = r * r
            s = r * horner(r2, SIN)
            E[pl.ds(rows, PTS), cols] = (1.0 - s * s).astype(BF16)
            E[pl.ds(pl.multiple_of(rows + 2048, PTS), PTS), cols] = (s * horner(r2, COS)).astype(BF16)
        for i, steps in E_STEPS.items():
            if steps:
                @pl.when(it == i)
                def _():
                    for ch, st in steps:
                        gstep(ch, st)

    xn, xp, other = dev(up(x, 1), y, c, z), dev(up(x, -1), y, c, z), dev(x, y, 1 - c, z)

    def core_copy(m):
        return remote(Po.at[m], Cx.at[m], cxs.at[m], cxr.at[m], other)

    def half_copy(ch, n):
        land, to = ((Hp, xn), (Hm, xp))[n]
        k = n * NCH + ch
        return remote(Pm.at[ch * 4, pl.ds(64 * n, 64)], land.at[ch], hs.at[k], hr.at[k], to)

    def full_copy(ch, n):
        land, to = ((Rp, xn), (Rm, xp))[n]
        k = n * NCH + ch
        return remote(Pm.at[ch * 4 + 1 + n], land.at[ch], rs.at[k], rr.at[k], to)

    def after_core(m):
        core_copy(m).wait_recv()
        Pm[m] = Pm[m] + Cx[m]
        ch, t = m // 4, lax.rem(m, 4)

        @pl.when(t == 0)
        def _():
            half_copy(ch, 0).start()
            half_copy(ch, 1).start()

        @pl.when(t == 1)
        def _():
            half_copy(ch, 0).wait_recv()
            Pm[m, 0:64] = Pm[m, 0:64] + Hp[ch]
            full_copy(ch, 0).start()

        @pl.when(t == 2)
        def _():
            half_copy(ch, 1).wait_recv()
            Pm[m, 64:128] = Pm[m, 64:128] + Hm[ch]
            full_copy(ch, 1).start()

    def finish(ch):
        full_copy(ch, 0).wait_recv()
        full_copy(ch, 1).wait_recv()
        res = Pm[ch * 4 + 3] + Rp[ch] + Rm[ch]
        out[pl.ds(pl.multiple_of(ch * HB, HB), HB), :] = res[0:64]
        out[pl.ds(pl.multiple_of(256 + ch * HB, HB), HB), :] = res[64:128]

    @pl.loop(0, 4 * NCH)
    def _(m):
        ch, t = m // 4, lax.rem(m, 4)

        @pl.when(t == 0)
        def _():
            for b in range(16):
                g = G[ch, b // N, b % N]
                lo, hi = g[0:64].astype(BF16), g[64:128].astype(BF16)
                cols, cols2 = slice(b * PTS, (b + 1) * PTS), slice(2048 + b * PTS, 2048 + (b + 1) * PTS)
                L[0:64, cols] = lo
                L[0:64, cols2] = hi
                L[64:128, cols] = hi
                L[64:128, cols2] = -lo

        part = jnp.dot(L[...], E[:, pl.ds(pl.multiple_of(t * 512, 512), 512)], preferred_element_type=F32)
        Pm[m] = part[:, :BLK]
        Po[m] = part[:, BLK:]
        core_copy(m).start()
        for i, steps in M_STEPS.items():
            @pl.when(m == i)
            def _():
                for ch_, st in steps:
                    gstep(ch_, st)

        @pl.when(m > 0)
        def _():
            after_core(m - 1)

        @pl.when((t == 2) & (m > 4))
        def _():
            finish(ch - 1)

    after_core(4 * NCH - 1)
    finish(NCH - 1)

    for d in n1 + n2 + [dc] + dsh + dg:
        d.wait_send()
    for ch in range(NCH):
        for st in range(4):
            for d in gcopies(ch, st):
                d.wait_send()
        for n in range(2):
            half_copy(ch, n).wait_send()
            full_copy(ch, n).wait_send()
        for t in range(4):
            core_copy(ch * 4 + t).wait_send()


def local(densities, weights, coords, counts, wave):
    vm = pl.BlockSpec(memory_space=pltpu.VMEM)
    dma = pltpu.SemaphoreType.DMA
    out = pl.pallas_call(
        kernel,
        out_shape=jax.ShapeDtypeStruct((512, BLK), F32),
        in_specs=[vm, vm, vm, pl.BlockSpec(memory_space=pltpu.SMEM), vm],
        out_specs=vm,
        scratch_shapes=[
            pltpu.VMEM((8, 8, 128), I32),
            pltpu.VMEM((16, 8, 128), I32),
            pltpu.VMEM((17, 8, 128), F32),
            pltpu.VMEM((8, 256), F32),
            pltpu.VMEM((8, 128), F32),
            pltpu.VMEM((8, NDIR), F32),
            pltpu.VMEM((128, NDIR), BF16),
            pltpu.VMEM((NCH, 128, 128), F32),
            pltpu.VMEM((NCH, 128, 128), F32),
            pltpu.VMEM((NCH, 128, 128), F32),
            pltpu.VMEM((NCH, N, N, 128, 128), F32),
            pltpu.VMEM((4096, NDIR), BF16),
            pltpu.VMEM((128, 4096), BF16),
            pltpu.VMEM((16, 128, BLK), F32),
            pltpu.VMEM((16, 128, BLK), F32),
            pltpu.VMEM((16, 128, BLK), F32),
            pltpu.VMEM((NCH, 64, BLK), F32),
            pltpu.VMEM((NCH, 64, BLK), F32),
            pltpu.VMEM((NCH, 128, BLK), F32),
            pltpu.VMEM((NCH, 128, BLK), F32),
            dma((7,)), dma((7,)),
            dma((15,)), dma((15,)),
            dma((1,)), dma((1,)),
            dma((15,)), dma((15,)),
            dma((NCH,)), dma((NCH,)),
            dma((NCH, 16)), dma((NCH, 16)),
            dma((16,)), dma((16,)),
            dma((2 * NCH,)), dma((2 * NCH,)),
            dma((2 * NCH,)), dma((2 * NCH,)),
        ],
        compiler_params=pltpu.CompilerParams(
            collective_id=0, has_side_effects=True, vmem_limit_bytes=56 * 2**20
        ),
        cost_estimate=pl.CostEstimate(flops=8_600_000_000, bytes_accessed=2_000_000, transcendentals=0),
        name="far_field",
    )(densities, weights.reshape(1, -1), coords, counts, wave)
    return out[:, None, :]


def solution(mesh):
    placed = (
        P(None, ("surf", "dir")),
        P(("surf", "dir")),
        P(None, ("surf", "dir")),
        P(("surf", "dir")),
        P(None, "dir", None),
    )
    return jax.shard_map(
        local, mesh=mesh, in_specs=placed, out_specs=P(None, "dir", "surf"), check_vma=False
    )
```

```python
import functools
import math

import numpy as np

import jax
import jax.numpy as jnp
from jax import lax
from jax.experimental import pallas as pl
from jax.experimental.pallas import tpu as pltpu
from jax.sharding import PartitionSpec as P

MESH = pl.DeviceIdType.MESH
F32, BF16, I32 = jnp.float32, jnp.bfloat16, jnp.int32
N = 4
PTS = 128
NCH = 4
HB = 64
NDIR = 2048
BLK = 256


def _fit(f, terms, odd):
    x = np.cos(np.linspace(0, np.pi / 2, 2001)) * 0.5
    a = np.stack([x ** (2 * k + odd) for k in range(terms)], 1)
    w = np.ones_like(x)
    for _ in range(60):
        c = np.linalg.lstsq(a * w[:, None], f(x) * w, rcond=None)[0]
        e = np.abs(a @ c - f(x))
        w = w * np.sqrt(e / e.max() + 0.02)
        w = w / w.max()
    return [float(np.float32(v)) for v in c * math.sqrt(2.0)]


SIN = _fit(lambda r: np.sin(np.pi * r), 3, 1)
COS = _fit(lambda r: np.cos(np.pi * r), 4, 0)


def horner(q, c):
    acc = c[-1] * q + c[-2]
    for k in c[-3::-1]:
        acc = acc * q + k
    return acc


def split3(v):
    a = v.astype(BF16).astype(F32)
    b = (v - a).astype(BF16).astype(F32)
    return a, b, (v - a) - b


E_STEPS = {
    1: [(0, 0)], 2: [(1, 0)], 3: [(2, 0)], 4: [(0, 1), (3, 0)], 5: [(1, 1)], 6: [(0, 2), (2, 1)], 7: [(3, 1)], 8: [(1, 2)],
    11: [(0, 3)], 12: [(2, 2)], 14: [(1, 3)], 15: [(0, 4), (3, 2)],
}
M_STEPS = {2: [(2, 3)], 3: [(1, 4)], 6: [(3, 3)], 7: [(2, 4)], 11: [(3, 4)]}


def kernel(
    dens_h, wts_h, coords_h, counts, wave_h, out,
    dens, wts, coords, wave, W, cnt1, cnt2, raw, shv, cnv, kf, kmat, X, keep, sout, sin_, G, E0, E1, E2, E3, L, Pm, Po, Cx,
    Hp, Hm, Rp, Rm,
    ins, s1s, s1r, s2s, s2r, sgs, sgr, sxs, sxr, shs, shr, ggs, ggr, cxs, cxr, hs, hr, rs, rr,
):
    E = (E0, E1, E2, E3)
    surf, z = lax.axis_index("surf"), lax.axis_index("dir")
    x, y, c = surf // 8, (surf // 2) % N, surf % 2
    q = surf * N + z

    def dev(xx, yy, cc, zz):
        return ((xx * N + yy) * 2 + cc, zz)

    def up(v, k):
        return lax.rem(v + (k + N), N)

    def remote(src, dst, ss, rs_, to):
        return pltpu.make_async_remote_copy(
            src_ref=src, dst_ref=dst, send_sem=ss, recv_sem=rs_, device_id=to, device_id_type=MESH
        )

    me8 = c * N + z
    peers8 = []
    for k in range(1, 8):
        o = lax.rem(me8 + k, 8)
        peers8.append(dev(x, y, o // N, lax.rem(o, N)))
    peers16 = [dev(up(x, i), up(y, j), c, z) for i in range(N) for j in range(N) if i or j]
    peersyz = [(i, j) for i in range(N) for j in range(N) if i or j]
    qn = lax.rem(q + 1, 128)
    nxt = (qn // N, lax.rem(qn, N))
    run = lax.rem(surf + 1, 32)
    runx, runy, runc = run // 8, (run // 2) % N, run % 2
    group = [dev(runx, i, runc, j) for i in range(N) for j in range(N)]
    ends = [(lax.rem((x * N + i) * 2 + c + 31, 32), N - 1) for i in range(N)]

    barrier = pltpu.get_barrier_semaphore()
    extra = [dev(x, up(y, i), c, up(z, j)) for i, j in peersyz if i and j]
    greet = peers8 + peers16 + extra + ends
    heard = len(greet) - N + jnp.where(z == N - 1, N * N, 0)
    for to in greet:
        pl.semaphore_signal(barrier, inc=1, device_id=to, device_id_type=MESH)
    fetch = [
        pltpu.make_async_copy(a, b, ins.at[k])
        for k, (a, b) in enumerate(((dens_h, dens), (wts_h, wts), (coords_h, coords), (wave_h, wave)))
    ]
    for d in fetch:
        d.start()
    cnt = counts[0]
    own = y * N + z
    raw[own] = jnp.zeros((8, 256), F32)
    cnt1[me8] = jnp.full((8, 128), cnt, I32)
    pl.semaphore_wait(barrier, heard)

    n1 = [
        remote(cnt1.at[me8], cnt1.at[me8], s1s.at[k], s1r.at[k], peers8[k]) for k in range(7)
    ]
    for d in n1:
        d.start()

    for d in fetch:
        d.wait()
    scale = 1.0 / math.sqrt(PTS * 128)
    w = wts[...]
    for ch in range(NCH):
        W[ch, 0:HB] = ((w * dens[ch * HB : (ch + 1) * HB, :]) * scale).astype(BF16)
        W[ch, HB:] = ((w * dens[256 + ch * HB : 256 + (ch + 1) * HB, :]) * scale).astype(BF16)
    kf[...] = jnp.zeros_like(kf)
    for t, dx in enumerate((2, 1, 3, 0)):
        for h in range(2):
            cc = c if h == 0 else 1 - c
            at = pl.multiple_of((up(x, dx) * 8 + y * 2 + cc) * BLK, BLK)
            for k in range(3):
                kf[k : k + 1, t * 512 + h * BLK : t * 512 + (h + 1) * BLK] = (
                    wave[k, :, pl.ds(at, BLK)] * (1.0 / (2.0 * math.pi))
                )
    k1, k2, k3 = split3(kf[...])
    kmat[...] = jnp.concatenate([k1, k2, k1, k3, k2, k1, jnp.zeros((80, NDIR), F32)], 0).astype(BF16)

    for d in n1:
        d.wait_recv()
    eight = jnp.zeros((8, 128), I32)
    line = lax.broadcasted_iota(I32, (8, 128), 0)
    for k in range(8):
        eight = jnp.where(line == k, cnt1[k], eight)
    me16 = x * N + y
    cnt2[me16] = eight
    n2 = [
        remote(cnt2.at[me16], cnt2.at[me16], s2s.at[k], s2r.at[k], peers16[k]) for k in range(15)
    ]
    for d in n2:
        d.start()

    raw[own, 0:3] = coords[...]
    dg = [
        remote(raw.at[own], raw.at[own], sgs.at[k], sgr.at[k], dev(x, up(y, i), c, up(z, j)))
        for k, (i, j) in enumerate(peersyz)
    ]
    for d in dg:
        d.start()

    def end_copy(k):
        return remote(raw.at[own], raw.at[16 + runy], sxs.at[k], sxr.at[runy], group[k])

    @pl.when(z == N - 1)
    def _():
        for k in range(16):
            end_copy(k).start()

    for d in n2:
        d.wait_recv()
    nums = cnt2[...].reshape(128, 128).astype(F32)
    at_row = lax.broadcasted_iota(I32, (128, 128), 0)
    at_col = lax.broadcasted_iota(I32, (128, 128), 1)
    lower = jnp.where(at_col < at_row, 1.0, 0.0).astype(BF16)
    cnv[...] = nums
    shv[...] = jnp.dot(lower, nums.astype(BF16), preferred_element_type=F32) - (at_row * PTS).astype(F32)

    def wide(row):
        return jnp.concatenate([row, row], 1)

    slot = lax.broadcasted_iota(I32, (256, 256), 0).astype(F32)
    col = lax.broadcasted_iota(I32, (256, 256), 1).astype(F32)
    myshift, mycnt = wide(shv[pl.ds(q, 1), :]), wide(cnv[pl.ds(q, 1), :])
    pick = jnp.where((col - slot == myshift) & (slot < mycnt), 1.0, 0.0).astype(BF16)

    dsh = [remote(sout.at[ch], sin_.at[ch], shs.at[ch], shr.at[ch], nxt) for ch in range(NCH)]

    def pack(ch):
        moved = jnp.dot(W[ch], pick, preferred_element_type=F32)
        keep[ch] = moved[:, :128]
        sout[ch] = moved[:, 128:]
        dsh[ch].start()

    for ch in range(NCH):
        pack(ch)

    def gcopies(ch, st):
        sem = lambda n: (ggs.at[ch, st * 4 + n], ggr.at[ch, st * 4 + n])
        yn, yp, zn, zp = (dev(x, up(y, 1), c, z), dev(x, up(y, -1), c, z), dev(x, y, c, up(z, 1)), dev(x, y, c, up(z, -1)))
        ym, yq, zm, zq = up(y, -1), up(y, 1), up(z, -1), up(z, 1)
        lo, lo1, lo2 = pl.ds(0, 64), pl.ds(0, 32), pl.ds(32, 32)
        hi, hi1, hi2 = pl.ds(64, 64), pl.ds(64, 32), pl.ds(96, 32)
        al = pl.ds(0, N)
        if st == 0:
            parts = [((y, z, lo), yn), ((y, z, lo), yp), ((y, z, hi), zn), ((y, z, hi), zp)]
        elif st == 1:
            parts = [((ym, z, lo1), yn), ((yq, z, lo2), yp), ((y, zm, hi1), zn), ((y, zq, hi2), zp)]
        elif st == 2:
            parts = [((al, z, lo), zn), ((al, z, lo), zp), ((y, al, hi), yn), ((y, al, hi), yp)]
        else:
            parts = [((al, zm, lo1), zn), ((al, zq, lo2), zp), ((ym, al, hi1), yn), ((yq, al, hi2), yp)]
        return [remote(G.at[(ch,) + p], G.at[(ch,) + p], *sem(n), to) for n, (p, to) in enumerate(parts)]

    def gstep(ch, st):
        if st == 0:
            dsh[ch].wait_recv()
            G[ch, y, z] = keep[ch] + sin_[ch]
        else:
            for d in gcopies(ch, st - 1):
                d.wait_recv()
        if st < 4:
            for d in gcopies(ch, st):
                d.start()

    for d in dg:
        d.wait_recv()
    for k in range(N):
        remote(raw.at[own], raw.at[16 + k], sxs.at[k], sxr.at[k], group[0]).wait_recv()

    slot_l = lax.broadcasted_iota(I32, (PTS, 256), 1).astype(F32)
    pos = lax.broadcasted_iota(I32, (PTS, 256), 0).astype(F32)

    def terms(k):
        a1, a2, a3 = split3(raw[k])
        return jnp.concatenate([a1, a1, a2, a1, a2, a3, jnp.zeros((80, 256), F32)], 0).astype(BF16)

    def chosen(dev_q, first):
        off, num = wide(shv[pl.ds(dev_q, 1), :]), wide(cnv[pl.ds(dev_q, 1), :])
        return jnp.where((pos + first - slot_l == off) & (slot_l < num), 1.0, 0.0).astype(BF16)

    def placed(yy, zz):
        qb = ((x * N + yy) * 2 + c) * N + zz
        ahead = 16 + yy if zz == 0 else yy * N + zz - 1
        dims = (((1,), (1,)), ((), ()))
        kept = lax.dot_general(chosen(qb, 0.0), terms(yy * N + zz), dims, preferred_element_type=F32)
        came = lax.dot_general(
            chosen(lax.rem(qb + 127, 128), 128.0), terms(ahead), dims, preferred_element_type=F32
        )
        return (kept + came).astype(BF16)

    def waves(t, i):
        yy = up(y, i)
        for h in range(2):
            rows = pl.multiple_of(yy * 512 + h * 256, 256)
            if t == 0:
                for k in range(2):
                    X[pl.ds(pl.multiple_of(rows + k * PTS, PTS), PTS), :] = placed(yy, h * 2 + k)
            xm = X[pl.ds(rows, 256), :]
            for j in range(2):
                cols = slice(j * 256, (j + 1) * 256)
                turn = jnp.dot(xm, kmat[:, t * 512 + j * 256 : t * 512 + (j + 1) * 256], preferred_element_type=F32)
                r = turn - jnp.round(turn)
                r2 = r * r
                s = r * horner(r2, SIN)
                E[t][pl.ds(rows, 256), cols] = (1.0 - s * s).astype(BF16)
                E[t][pl.ds(pl.multiple_of(rows + 2048, 256), 256), cols] = (s * horner(r2, COS)).astype(BF16)

    def wave_loop(t):
        @pl.loop(0, 4)
        def _(i):
            waves(t, i)
            for k in range(4):
                steps = E_STEPS.get(t * 4 + k, [])
                if steps:
                    @pl.when(i == k)
                    def _():
                        for ch, st in steps:
                            gstep(ch, st)

    xn, xp, other = dev(up(x, 1), y, c, z), dev(up(x, -1), y, c, z), dev(x, y, 1 - c, z)

    def core_copy(ch, t):
        m = ch * 4 + t
        return remote(Po.at[m], Cx.at[m], cxs.at[m], cxr.at[m], other)

    def half_copy(ch, n):
        land, to = ((Hp, xn), (Hm, xp))[n]
        k = n * NCH + ch
        return remote(Pm.at[ch * 4, pl.ds(64 * n, 64)], land.at[ch], hs.at[k], hr.at[k], to)

    def full_copy(ch, n):
        land, to = ((Rp, xn), (Rm, xp))[n]
        k = n * NCH + ch
        return remote(Pm.at[ch * 4 + 1 + n], land.at[ch], rs.at[k], rr.at[k], to)

    def core_done(ch, t):
        core_copy(ch, t).wait_recv()
        m = ch * 4 + t
        Pm[m] = Pm[m] + Cx[m]
        if t == 0:
            half_copy(ch, 0).start()
            half_copy(ch, 1).start()

    def forward(ch):
        for n in range(2):
            half_copy(ch, n).wait_recv()
            here = pl.ds(64 * n, 64)
            Pm[ch * 4 + 1 + n, here] = Pm[ch * 4 + 1 + n, here] + (Hp, Hm)[n][ch]
            full_copy(ch, n).start()

    def finish(ch):
        full_copy(ch, 0).wait_recv()
        full_copy(ch, 1).wait_recv()
        res = Pm[ch * 4 + 3] + Rp[ch] + Rm[ch]
        out[pl.ds(pl.multiple_of(ch * HB, HB), HB), :] = res[0:64]
        out[pl.ds(pl.multiple_of(256 + ch * HB, HB), HB), :] = res[64:128]

    def build(ch):
        for b in range(16):
            g = G[ch, b // N, b % N]
            lo, hi = g[0:64].astype(BF16), g[64:128].astype(BF16)
            cols, cols2 = slice(b * PTS, (b + 1) * PTS), slice(2048 + b * PTS, 2048 + (b + 1) * PTS)
            L[0:64, cols] = lo
            L[0:64, cols2] = hi
            L[64:128, cols] = hi
            L[64:128, cols2] = -lo

    def product(ch, t):
        part = jnp.dot(L[...], E[t][...], preferred_element_type=F32)
        Pm[ch * 4 + t] = part[:, :BLK]
        Po[ch * 4 + t] = part[:, BLK:]
        core_copy(ch, t).start()

    def m_steps(m):
        for ch, st in M_STEPS.get(m, []):
            gstep(ch, st)

    for t in range(4):
        wave_loop(t)

    @pl.loop(0, NCH)
    def _(ch):
        build(ch)
        for t in range(4):
            product(ch, t)
            if t < 2:
                @pl.when(ch > 0)
                def _():
                    core_done(ch - 1, t + 2)
            else:
                core_done(ch, t - 2)
            if t == 2:
                @pl.when(ch > 0)
                def _():
                    forward(ch - 1)
            for k in range(NCH):
                if k * 4 + t in M_STEPS:
                    @pl.when(ch == k)
                    def _():
                        m_steps(k * 4 + t)

    core_done(NCH - 1, 2)
    core_done(NCH - 1, 3)
    forward(NCH - 1)
    for ch in range(NCH):
        finish(ch)

    for d in n1 + n2 + dsh + dg:
        d.wait_send()

    @pl.when(z == N - 1)
    def _():
        for k in range(16):
            end_copy(k).wait_send()

    for ch in range(NCH):
        for st in range(4):
            for d in gcopies(ch, st):
                d.wait_send()
        for n in range(2):
            half_copy(ch, n).wait_send()
            full_copy(ch, n).wait_send()
        for t in range(4):
            core_copy(ch, t).wait_send()


def local(densities, weights, coords, counts, wave):
    vm, hbm = pl.BlockSpec(memory_space=pltpu.VMEM), pl.BlockSpec(memory_space=pl.ANY)
    dma = pltpu.SemaphoreType.DMA
    out = pl.pallas_call(
        kernel,
        out_shape=jax.ShapeDtypeStruct((512, BLK), F32),
        in_specs=[hbm, hbm, hbm, pl.BlockSpec(memory_space=pltpu.SMEM), hbm],
        out_specs=vm,
        scratch_shapes=[
            pltpu.VMEM((512, 256), F32),
            pltpu.VMEM((1, 256), F32),
            pltpu.VMEM((3, 256), F32),
            pltpu.VMEM((3, 1, 8192), F32),
            pltpu.VMEM((NCH, 128, 256), BF16),
            pltpu.VMEM((8, 8, 128), I32),
            pltpu.VMEM((16, 8, 128), I32),
            pltpu.VMEM((20, 8, 256), F32),
            pltpu.VMEM((128, 128), F32),
            pltpu.VMEM((128, 128), F32),
            pltpu.VMEM((8, NDIR), F32),
            pltpu.VMEM((128, NDIR), BF16),
            pltpu.VMEM((2048, 128), BF16),
            pltpu.VMEM((NCH, 128, 128), F32),
            pltpu.VMEM((NCH, 128, 128), F32),
            pltpu.VMEM((NCH, 128, 128), F32),
            pltpu.VMEM((NCH, N, N, 128, 128), F32),
            pltpu.VMEM((4096, 512), BF16),
            pltpu.VMEM((4096, 512), BF16),
            pltpu.VMEM((4096, 512), BF16),
            pltpu.VMEM((4096, 512), BF16),
            pltpu.VMEM((128, 4096), BF16),
            pltpu.VMEM((16, 128, BLK), F32),
            pltpu.VMEM((16, 128, BLK), F32),
            pltpu.VMEM((16, 128, BLK), F32),
            pltpu.VMEM((NCH, 64, BLK), F32),
            pltpu.VMEM((NCH, 64, BLK), F32),
            pltpu.VMEM((NCH, 128, BLK), F32),
            pltpu.VMEM((NCH, 128, BLK), F32),
            dma((4,)),
            dma((7,)), dma((7,)),
            dma((15,)), dma((15,)),
            dma((15,)), dma((15,)),
            dma((16,)), dma((N,)),
            dma((NCH,)), dma((NCH,)),
            dma((NCH, 16)), dma((NCH, 16)),
            dma((16,)), dma((16,)),
            dma((2 * NCH,)), dma((2 * NCH,)),
            dma((2 * NCH,)), dma((2 * NCH,)),
        ],
        compiler_params=pltpu.CompilerParams(
            collective_id=0, has_side_effects=True, vmem_limit_bytes=56 * 2**20
        ),
        cost_estimate=pl.CostEstimate(flops=8_600_000_000, bytes_accessed=2_000_000, transcendentals=0),
        name="far_field",
    )(densities, weights.reshape(1, -1), coords, counts, wave)
    return out[:, None, :]


def solution(mesh):
    placed = (
        P(None, ("surf", "dir")),
        P(("surf", "dir")),
        P(None, ("surf", "dir")),
        P(("surf", "dir")),
        P(None, "dir", None),
    )
    return jax.shard_map(
        local, mesh=mesh, in_specs=placed, out_specs=P(None, "dir", "surf"), check_vma=False
    )
```

```python
import functools
import math

import numpy as np

import jax
import jax.numpy as jnp
from jax import lax
from jax.experimental import pallas as pl
from jax.experimental.pallas import tpu as pltpu
from jax.sharding import PartitionSpec as P

MESH = pl.DeviceIdType.MESH
F32, BF16, I32 = jnp.float32, jnp.bfloat16, jnp.int32
N = 4
PTS = 128
NCH = 4
HB = 64
NDIR = 2048
BLK = 256


def _fit(f, terms, odd):
    x = np.cos(np.linspace(0, np.pi / 2, 2001)) * 0.5
    a = np.stack([x ** (2 * k + odd) for k in range(terms)], 1)
    w = np.ones_like(x)
    for _ in range(60):
        c = np.linalg.lstsq(a * w[:, None], f(x) * w, rcond=None)[0]
        e = np.abs(a @ c - f(x))
        w = w * np.sqrt(e / e.max() + 0.02)
        w = w / w.max()
    return [float(np.float32(v)) for v in c * math.sqrt(2.0)]


SIN = _fit(lambda r: np.sin(np.pi * r), 3, 1)
COS = _fit(lambda r: np.cos(np.pi * r), 4, 0)


def horner(q, c):
    acc = c[-1] * q + c[-2]
    for k in c[-3::-1]:
        acc = acc * q + k
    return acc


def split3(v):
    a = v.astype(BF16).astype(F32)
    b = (v - a).astype(BF16).astype(F32)
    return a, b, (v - a) - b


E_STEPS = {
    1: [(0, 0)], 2: [(1, 0)], 3: [(2, 0)], 4: [(0, 1), (3, 0)], 5: [(1, 1)], 6: [(0, 2), (2, 1)], 7: [(3, 1)], 8: [(1, 2)],
    11: [(0, 3)], 12: [(2, 2)], 14: [(1, 3)], 15: [(0, 4), (3, 2)],
}
M_STEPS = {2: [(2, 3)], 3: [(1, 4)], 6: [(3, 3)], 7: [(2, 4)], 11: [(3, 4)]}


def kernel(
    dens_h, wts_h, coords_h, counts, wave_h, out,
    dens, wts, coords, wave, W, cnt1, cnt2, raw, shv, cnv, kf, kmat, X, keep, sout, sin_, G, E, L, Pm, Po, Cx,
    Hp, Hm, Rp, Rm,
    ins, s1s, s1r, s2s, s2r, sgs, sgr, sxs, sxr, shs, shr, ggs, ggr, cxs, cxr, hs, hr, rs, rr,
):
    surf, z = lax.axis_index("surf"), lax.axis_index("dir")
    x, y, c = surf // 8, (surf // 2) % N, surf % 2
    q = surf * N + z

    def dev(xx, yy, cc, zz):
        return ((xx * N + yy) * 2 + cc, zz)

    def up(v, k):
        return lax.rem(v + (k + N), N)

    def remote(src, dst, ss, rs_, to):
        return pltpu.make_async_remote_copy(
            src_ref=src, dst_ref=dst, send_sem=ss, recv_sem=rs_, device_id=to, device_id_type=MESH
        )

    me8 = c * N + z
    peers8 = []
    for k in range(1, 8):
        o = lax.rem(me8 + k, 8)
        peers8.append(dev(x, y, o // N, lax.rem(o, N)))
    peers16 = [dev(up(x, i), up(y, j), c, z) for i in range(N) for j in range(N) if i or j]
    peersyz = [(i, j) for i in range(N) for j in range(N) if i or j]
    qn = lax.rem(q + 1, 128)
    nxt = (qn // N, lax.rem(qn, N))
    run = lax.rem(surf + 1, 32)
    runx, runy, runc = run // 8, (run // 2) % N, run % 2
    group = [dev(runx, i, runc, j) for i in range(N) for j in range(N)]

    barrier = pltpu.get_barrier_semaphore()
    greet = peers8 + peers16
    for to in greet:
        pl.semaphore_signal(barrier, inc=1, device_id=to, device_id_type=MESH)
    fetch = [
        pltpu.make_async_copy(a, b, ins.at[k])
        for k, (a, b) in enumerate(((dens_h, dens), (wts_h, wts), (coords_h, coords), (wave_h, wave)))
    ]
    for d in fetch:
        d.start()
    cnt = counts[0]
    own = y * N + z
    raw[own] = jnp.zeros((8, 256), F32)
    cnt1[me8] = jnp.full((8, 128), cnt, I32)
    pl.semaphore_wait(barrier, len(greet))

    n1 = [
        remote(cnt1.at[me8], cnt1.at[me8], s1s.at[k], s1r.at[k], peers8[k]) for k in range(7)
    ]
    for d in n1:
        d.start()

    for d in fetch:
        d.wait()
    scale = 1.0 / math.sqrt(PTS * 128)
    w = wts[...]
    for ch in range(NCH):
        W[ch, 0:HB] = ((w * dens[ch * HB : (ch + 1) * HB, :]) * scale).astype(BF16)
        W[ch, HB:] = ((w * dens[256 + ch * HB : 256 + (ch + 1) * HB, :]) * scale).astype(BF16)
    kf[...] = jnp.zeros_like(kf)
    for t, dx in enumerate((2, 1, 3, 0)):
        for h in range(2):
            cc = c if h == 0 else 1 - c
            at = pl.multiple_of((up(x, dx) * 8 + y * 2 + cc) * BLK, BLK)
            for k in range(3):
                kf[k : k + 1, t * 512 + h * BLK : t * 512 + (h + 1) * BLK] = (
                    wave[k, :, pl.ds(at, BLK)] * (1.0 / (2.0 * math.pi))
                )
    k1, k2, k3 = split3(kf[...])
    turns = jnp.concatenate([k1, k2, k1, k3, k2, k1, jnp.zeros((80, NDIR), F32)], 0).astype(BF16)
    for t in range(4):
        kmat[t] = turns[:, t * 512 : (t + 1) * 512]

    for d in n1:
        d.wait_recv()
    eight = jnp.zeros((8, 128), I32)
    line = lax.broadcasted_iota(I32, (8, 128), 0)
    for k in range(8):
        eight = jnp.where(line == k, cnt1[k], eight)
    me16 = x * N + y
    cnt2[me16] = eight
    n2 = [
        remote(cnt2.at[me16], cnt2.at[me16], s2s.at[k], s2r.at[k], peers16[k]) for k in range(15)
    ]
    for d in n2:
        d.start()

    raw[own, 0:3] = coords[...]
    dg = [
        remote(raw.at[own], raw.at[own], sgs.at[k], sgr.at[k], dev(x, up(y, i), c, up(z, j)))
        for k, (i, j) in enumerate(peersyz)
    ]
    for d in dg:
        d.start()

    def end_copy(k):
        return remote(raw.at[own], raw.at[16 + runy], sxs.at[k], sxr.at[runy], group[k])

    @pl.when(z == N - 1)
    def _():
        for k in range(16):
            end_copy(k).start()

    for d in n2:
        d.wait_recv()
    nums = cnt2[...].reshape(128, 128).astype(F32)
    at_row = lax.broadcasted_iota(I32, (128, 128), 0)
    at_col = lax.broadcasted_iota(I32, (128, 128), 1)
    lower = jnp.where(at_col < at_row, 1.0, 0.0).astype(BF16)
    cnv[...] = nums
    shv[...] = jnp.dot(lower, nums.astype(BF16), preferred_element_type=F32) - (at_row * PTS).astype(F32)

    def wide(row):
        return jnp.concatenate([row, row], 1)

    slot = lax.broadcasted_iota(I32, (256, 256), 0).astype(F32)
    col = lax.broadcasted_iota(I32, (256, 256), 1).astype(F32)
    myshift, mycnt = wide(shv[pl.ds(q, 1), :]), wide(cnv[pl.ds(q, 1), :])
    pick = jnp.where((col - slot == myshift) & (slot < mycnt), 1.0, 0.0).astype(BF16)

    dsh = [remote(sout.at[ch], sin_.at[ch], shs.at[ch], shr.at[ch], nxt) for ch in range(NCH)]

    def pack(ch):
        moved = jnp.dot(W[ch], pick, preferred_element_type=F32)
        keep[ch] = moved[:, :128]
        sout[ch] = moved[:, 128:]
        dsh[ch].start()

    for ch in range(NCH):
        pack(ch)

    def gcopies(ch, st):
        sem = lambda n: (ggs.at[ch, st * 4 + n], ggr.at[ch, st * 4 + n])
        yn, yp, zn, zp = (dev(x, up(y, 1), c, z), dev(x, up(y, -1), c, z), dev(x, y, c, up(z, 1)), dev(x, y, c, up(z, -1)))
        ym, yq, zm, zq = up(y, -1), up(y, 1), up(z, -1), up(z, 1)
        lo, lo1, lo2 = pl.ds(0, 64), pl.ds(0, 32), pl.ds(32, 32)
        hi, hi1, hi2 = pl.ds(64, 64), pl.ds(64, 32), pl.ds(96, 32)
        al = pl.ds(0, N)
        if st == 0:
            parts = [((y, z, lo), yn), ((y, z, lo), yp), ((y, z, hi), zn), ((y, z, hi), zp)]
        elif st == 1:
            parts = [((ym, z, lo1), yn), ((yq, z, lo2), yp), ((y, zm, hi1), zn), ((y, zq, hi2), zp)]
        elif st == 2:
            parts = [((al, z, lo), zn), ((al, z, lo), zp), ((y, al, hi), yn), ((y, al, hi), yp)]
        else:
            parts = [((al, zm, lo1), zn), ((al, zq, lo2), zp), ((ym, al, hi1), yn), ((yq, al, hi2), yp)]
        return [remote(G.at[(ch,) + p], G.at[(ch,) + p], *sem(n), to) for n, (p, to) in enumerate(parts)]

    def gstep(ch, st):
        if st == 0:
            dsh[ch].wait_recv()
            G[ch, y, z] = keep[ch] + sin_[ch]
        else:
            for d in gcopies(ch, st - 1):
                d.wait_recv()
        if st < 4:
            for d in gcopies(ch, st):
                d.start()

    for d in dg:
        d.wait_recv()
    for k in range(N):
        remote(raw.at[own], raw.at[16 + k], sxs.at[k], sxr.at[k], group[0]).wait_recv()

    slot_l = lax.broadcasted_iota(I32, (PTS, 256), 1).astype(F32)
    pos = lax.broadcasted_iota(I32, (PTS, 256), 0).astype(F32)

    def terms(k):
        a1, a2, a3 = split3(raw[k])
        return jnp.concatenate([a1, a1, a2, a1, a2, a3, jnp.zeros((80, 256), F32)], 0).astype(BF16)

    def chosen(dev_q, first):
        off, num = wide(shv[pl.ds(dev_q, 1), :]), wide(cnv[pl.ds(dev_q, 1), :])
        return jnp.where((pos + first - slot_l == off) & (slot_l < num), 1.0, 0.0).astype(BF16)

    def placed(yy, zz):
        qb = ((x * N + yy) * 2 + c) * N + zz
        ahead = jnp.where(zz == 0, 16 + yy, yy * N + zz - 1)
        dims = (((1,), (1,)), ((), ()))
        kept = lax.dot_general(chosen(qb, 0.0), terms(yy * N + zz), dims, preferred_element_type=F32)
        came = lax.dot_general(
            chosen(lax.rem(qb + 127, 128), 128.0), terms(ahead), dims, preferred_element_type=F32
        )
        return (kept + came).astype(BF16)

    @pl.loop(0, 16)
    def _(b):
        yy, zz = b // N, lax.rem(b, N)
        X[pl.ds(pl.multiple_of(b * PTS, PTS), PTS), :] = placed(yy, zz)

    @pl.loop(0, 16)
    def _(it):
        t, i = it // 4, lax.rem(it, 4)
        for h in range(2):
            rows = pl.multiple_of(i * 512 + h * 256, 256)
            xm = X[pl.ds(rows, 256), :]
            for j in range(2):
                cols = slice(j * 256, (j + 1) * 256)
                turn = jnp.dot(xm, kmat[t, :, cols], preferred_element_type=F32)
                r = turn - jnp.round(turn)
                r2 = r * r
                s = r * horner(r2, SIN)
                E[t, pl.ds(rows, 256), cols] = (1.0 - s * s).astype(BF16)
                E[t, pl.ds(pl.multiple_of(rows + 2048, 256), 256), cols] = (s * horner(r2, COS)).astype(BF16)
        for k, steps in E_STEPS.items():
            @pl.when(it == k)
            def _():
                for ch, st in steps:
                    gstep(ch, st)

    xn, xp, other = dev(up(x, 1), y, c, z), dev(up(x, -1), y, c, z), dev(x, y, 1 - c, z)

    def core_copy(ch, t):
        m = ch * 4 + t
        return remote(Po.at[m], Cx.at[m], cxs.at[m], cxr.at[m], other)

    def half_copy(ch, n):
        land, to = ((Hp, xn), (Hm, xp))[n]
        k = n * NCH + ch
        return remote(Pm.at[ch * 4, pl.ds(64 * n, 64)], land.at[ch], hs.at[k], hr.at[k], to)

    def full_copy(ch, n):
        land, to = ((Rp, xn), (Rm, xp))[n]
        k = n * NCH + ch
        return remote(Pm.at[ch * 4 + 1 + n], land.at[ch], rs.at[k], rr.at[k], to)

    def core_done(ch, t):
        core_copy(ch, t).wait_recv()
        m = ch * 4 + t
        Pm[m] = Pm[m] + Cx[m]
        if t == 0:
            half_copy(ch, 0).start()
            half_copy(ch, 1).start()

    def forward(ch):
        for n in range(2):
            half_copy(ch, n).wait_recv()
            here = pl.ds(64 * n, 64)
            Pm[ch * 4 + 1 + n, here] = Pm[ch * 4 + 1 + n, here] + (Hp, Hm)[n][ch]
            full_copy(ch, n).start()

    def finish(ch):
        full_copy(ch, 0).wait_recv()
        full_copy(ch, 1).wait_recv()
        res = Pm[ch * 4 + 3] + Rp[ch] + Rm[ch]
        out[pl.ds(pl.multiple_of(ch * HB, HB), HB), :] = res[0:64]
        out[pl.ds(pl.multiple_of(256 + ch * HB, HB), HB), :] = res[64:128]

    def build(ch):
        for b in range(16):
            g = G[ch, b // N, b % N]
            lo, hi = g[0:64].astype(BF16), g[64:128].astype(BF16)
            cols, cols2 = slice(b * PTS, (b + 1) * PTS), slice(2048 + b * PTS, 2048 + (b + 1) * PTS)
            L[0:64, cols] = lo
            L[0:64, cols2] = hi
            L[64:128, cols] = hi
            L[64:128, cols2] = -lo

    def product(ch, t):
        part = jnp.dot(L[...], E[t], preferred_element_type=F32)
        Pm[ch * 4 + t] = part[:, :BLK]
        Po[ch * 4 + t] = part[:, BLK:]
        core_copy(ch, t).start()

    def m_steps(m):
        for ch, st in M_STEPS.get(m, []):
            gstep(ch, st)

    @pl.loop(0, 4 * NCH)
    def _(m):
        ch, t = m // 4, lax.rem(m, 4)

        @pl.when(t == 0)
        def _():
            build(ch)

        product(ch, t)
        for k in range(4):
            @pl.when((t == k) & (m > 1))
            def _():
                core_done(ch - (1 if k < 2 else 0), (k + 2) % 4)
                if k == 2:
                    @pl.when(ch > 0)
                    def _():
                        forward(ch - 1)
        for k in M_STEPS:
            @pl.when(m == k)
            def _():
                m_steps(k)

    core_done(NCH - 1, 2)
    core_done(NCH - 1, 3)
    forward(NCH - 1)
    for ch in range(NCH):
        finish(ch)

    for d in n1 + n2 + dsh + dg:
        d.wait_send()

    @pl.when(z == N - 1)
    def _():
        for k in range(16):
            end_copy(k).wait_send()

    for ch in range(NCH):
        for st in range(4):
            for d in gcopies(ch, st):
                d.wait_send()
        for n in range(2):
            half_copy(ch, n).wait_send()
            full_copy(ch, n).wait_send()
        for t in range(4):
            core_copy(ch, t).wait_send()


def local(densities, weights, coords, counts, wave):
    vm, hbm = pl.BlockSpec(memory_space=pltpu.VMEM), pl.BlockSpec(memory_space=pl.ANY)
    dma = pltpu.SemaphoreType.DMA
    out = pl.pallas_call(
        kernel,
        out_shape=jax.ShapeDtypeStruct((512, BLK), F32),
        in_specs=[hbm, hbm, hbm, pl.BlockSpec(memory_space=pltpu.SMEM), hbm],
        out_specs=vm,
        scratch_shapes=[
            pltpu.VMEM((512, 256), F32),
            pltpu.VMEM((1, 256), F32),
            pltpu.VMEM((3, 256), F32),
            pltpu.VMEM((3, 1, 8192), F32),
            pltpu.VMEM((NCH, 128, 256), BF16),
            pltpu.VMEM((8, 8, 128), I32),
            pltpu.VMEM((16, 8, 128), I32),
            pltpu.VMEM((20, 8, 256), F32),
            pltpu.VMEM((128, 128), F32),
            pltpu.VMEM((128, 128), F32),
            pltpu.VMEM((8, NDIR), F32),
            pltpu.VMEM((4, 128, 512), BF16),
            pltpu.VMEM((2048, 128), BF16),
            pltpu.VMEM((NCH, 128, 128), F32),
            pltpu.VMEM((NCH, 128, 128), F32),
            pltpu.VMEM((NCH, 128, 128), F32),
            pltpu.VMEM((NCH, N, N, 128, 128), F32),
            pltpu.VMEM((4, 4096, 512), BF16),
            pltpu.VMEM((128, 4096), BF16),
            pltpu.VMEM((16, 128, BLK), F32),
            pltpu.VMEM((16, 128, BLK), F32),
            pltpu.VMEM((16, 128, BLK), F32),
            pltpu.VMEM((NCH, 64, BLK), F32),
            pltpu.VMEM((NCH, 64, BLK), F32),
            pltpu.VMEM((NCH, 128, BLK), F32),
            pltpu.VMEM((NCH, 128, BLK), F32),
            dma((4,)),
            dma((7,)), dma((7,)),
            dma((15,)), dma((15,)),
            dma((15,)), dma((15,)),
            dma((16,)), dma((N,)),
            dma((NCH,)), dma((NCH,)),
            dma((NCH, 16)), dma((NCH, 16)),
            dma((16,)), dma((16,)),
            dma((2 * NCH,)), dma((2 * NCH,)),
            dma((2 * NCH,)), dma((2 * NCH,)),
        ],
        compiler_params=pltpu.CompilerParams(
            collective_id=0, has_side_effects=True, vmem_limit_bytes=56 * 2**20
        ),
        cost_estimate=pl.CostEstimate(flops=8_600_000_000, bytes_accessed=2_000_000, transcendentals=0),
        name="far_field",
    )(densities, weights.reshape(1, -1), coords, counts, wave)
    return out[:, None, :]


def solution(mesh):
    placed = (
        P(None, ("surf", "dir")),
        P(("surf", "dir")),
        P(None, ("surf", "dir")),
        P(("surf", "dir")),
        P(None, "dir", None),
    )
    return jax.shard_map(
        local, mesh=mesh, in_specs=placed, out_specs=P(None, "dir", "surf"), check_vma=False
    )
```

```python
import functools
import math

import numpy as np

import jax
import jax.numpy as jnp
from jax import lax
from jax.experimental import pallas as pl
from jax.experimental.pallas import tpu as pltpu
from jax.sharding import PartitionSpec as P

MESH = pl.DeviceIdType.MESH
F32, BF16, I32 = jnp.float32, jnp.bfloat16, jnp.int32
N = 4
PTS = 128
NCH = 4
HB = 64
NDIR = 2048
BLK = 256


def _fit(f, terms, odd):
    x = np.cos(np.linspace(0, np.pi / 2, 2001)) * 0.5
    a = np.stack([x ** (2 * k + odd) for k in range(terms)], 1)
    w = np.ones_like(x)
    for _ in range(60):
        c = np.linalg.lstsq(a * w[:, None], f(x) * w, rcond=None)[0]
        e = np.abs(a @ c - f(x))
        w = w * np.sqrt(e / e.max() + 0.02)
        w = w / w.max()
    return [float(np.float32(v)) for v in c * math.sqrt(2.0)]


SIN = _fit(lambda r: np.sin(np.pi * r), 3, 1)
COS = _fit(lambda r: np.cos(np.pi * r), 4, 0)


def horner(q, c):
    acc = c[-1] * q + c[-2]
    for k in c[-3::-1]:
        acc = acc * q + k
    return acc


def split3(v):
    a = v.astype(BF16).astype(F32)
    b = (v - a).astype(BF16).astype(F32)
    return a, b, (v - a) - b


E_STEPS = {1: [(0, 0)], 2: [(1, 0)], 3: [(2, 0)], 4: [(3, 0)], 5: [(0, 1)], 7: [(1, 1)], 10: [(0, 2)], 11: [(2, 1)], 13: [(1, 2)], 14: [(3, 1)], 15: [(0, 3)]}
M_STEPS = {2: [(2, 2)], 3: [(1, 3)], 6: [(3, 2)], 7: [(2, 3)], 11: [(3, 3)]}


def kernel(
    dens_h, wts_h, coords_h, counts, wave_h, out,
    dens, wts, coords, wave, W, cnt1, cnt2, raw, shv, cnv, kf, kmat, X, keep, sout, sin_, G, E, L, Pm, Po, Cx,
    Hp, Hm, Rp, Rm,
    ins, s1s, s1r, s2s, s2r, sgs, sgr, sxs, sxr, shs, shr, ggs, ggr, cxs, cxr, hs, hr, rs, rr,
):
    surf, z = lax.axis_index("surf"), lax.axis_index("dir")
    x, y, c = surf // 8, (surf // 2) % N, surf % 2
    q = surf * N + z

    def dev(xx, yy, cc, zz):
        return ((xx * N + yy) * 2 + cc, zz)

    def up(v, k):
        return lax.rem(v + (k + N), N)

    def remote(src, dst, ss, rs_, to):
        return pltpu.make_async_remote_copy(
            src_ref=src, dst_ref=dst, send_sem=ss, recv_sem=rs_, device_id=to, device_id_type=MESH
        )

    me8 = c * N + z
    peers8 = []
    for k in range(1, 8):
        o = lax.rem(me8 + k, 8)
        peers8.append(dev(x, y, o // N, lax.rem(o, N)))
    peers16 = [dev(up(x, i), up(y, j), c, z) for i in range(N) for j in range(N) if i or j]
    peersyz = [(i, j) for i in range(N) for j in range(N) if i or j]
    qn = lax.rem(q + 1, 128)
    nxt = (qn // N, lax.rem(qn, N))
    run = lax.rem(surf + 1, 32)
    runx, runy, runc = run // 8, (run // 2) % N, run % 2
    group = [dev(runx, i, runc, j) for i in range(N) for j in range(N)]

    barrier = pltpu.get_barrier_semaphore()
    greet = peers8 + peers16
    for to in greet:
        pl.semaphore_signal(barrier, inc=1, device_id=to, device_id_type=MESH)
    fetch = [
        pltpu.make_async_copy(a, b, ins.at[k])
        for k, (a, b) in enumerate(((dens_h, dens), (wts_h, wts), (coords_h, coords), (wave_h, wave)))
    ]
    for d in fetch:
        d.start()
    cnt = counts[0]
    own = y * N + z
    raw[own] = jnp.zeros((8, 256), F32)
    cnt1[me8] = jnp.full((8, 128), cnt, I32)
    pl.semaphore_wait(barrier, len(greet))

    n1 = [
        remote(cnt1.at[me8], cnt1.at[me8], s1s.at[k], s1r.at[k], peers8[k]) for k in range(7)
    ]
    for d in n1:
        d.start()

    for d in fetch:
        d.wait()
    scale = 1.0 / math.sqrt(PTS * 128)
    w = wts[...]
    for ch in range(NCH):
        W[ch, 0:HB] = ((w * dens[ch * HB : (ch + 1) * HB, :]) * scale).astype(BF16)
        W[ch, HB:] = ((w * dens[256 + ch * HB : 256 + (ch + 1) * HB, :]) * scale).astype(BF16)
    kf[...] = jnp.zeros_like(kf)
    for t, dx in enumerate((2, 1, 3, 0)):
        for h in range(2):
            cc = c if h == 0 else 1 - c
            at = pl.multiple_of((up(x, dx) * 8 + y * 2 + cc) * BLK, BLK)
            for k in range(3):
                kf[k : k + 1, t * 512 + h * BLK : t * 512 + (h + 1) * BLK] = (
                    wave[k, :, pl.ds(at, BLK)] * (1.0 / (2.0 * math.pi))
                )
    k1, k2, k3 = split3(kf[...])
    turns = jnp.concatenate([k1, k2, k1, k3, k2, k1, jnp.zeros((80, NDIR), F32)], 0).astype(BF16)
    for t in range(4):
        kmat[t] = turns[:, t * 512 : (t + 1) * 512]

    for d in n1:
        d.wait_recv()
    eight = jnp.zeros((8, 128), I32)
    line = lax.broadcasted_iota(I32, (8, 128), 0)
    for k in range(8):
        eight = jnp.where(line == k, cnt1[k], eight)
    me16 = x * N + y
    cnt2[me16] = eight
    n2 = [
        remote(cnt2.at[me16], cnt2.at[me16], s2s.at[k], s2r.at[k], peers16[k]) for k in range(15)
    ]
    for d in n2:
        d.start()

    raw[own, 0:3] = coords[...]
    dg = [
        remote(raw.at[own], raw.at[own], sgs.at[k], sgr.at[k], dev(x, up(y, i), c, up(z, j)))
        for k, (i, j) in enumerate(peersyz)
    ]
    for d in dg:
        d.start()

    def end_copy(k):
        return remote(raw.at[own], raw.at[16 + runy], sxs.at[k], sxr.at[runy], group[k])

    @pl.when(z == N - 1)
    def _():
        for k in range(16):
            end_copy(k).start()

    for d in n2:
        d.wait_recv()
    nums = cnt2[...].reshape(128, 128).astype(F32)
    at_row = lax.broadcasted_iota(I32, (128, 128), 0)
    at_col = lax.broadcasted_iota(I32, (128, 128), 1)
    lower = jnp.where(at_col < at_row, 1.0, 0.0).astype(BF16)
    cnv[...] = nums
    shv[...] = jnp.dot(lower, nums.astype(BF16), preferred_element_type=F32) - (at_row * PTS).astype(F32)

    def wide(row):
        return jnp.concatenate([row, row], 1)

    slot = lax.broadcasted_iota(I32, (256, 256), 0).astype(F32)
    col = lax.broadcasted_iota(I32, (256, 256), 1).astype(F32)
    myshift, mycnt = wide(shv[pl.ds(q, 1), :]), wide(cnv[pl.ds(q, 1), :])
    pick = jnp.where((col - slot == myshift) & (slot < mycnt), 1.0, 0.0).astype(BF16)

    dsh = [remote(sout.at[ch], sin_.at[ch], shs.at[ch], shr.at[ch], nxt) for ch in range(NCH)]

    def pack(ch):
        moved = jnp.dot(W[ch], pick, preferred_element_type=F32)
        keep[ch] = moved[:, :128]
        sout[ch] = moved[:, 128:]
        dsh[ch].start()

    for ch in range(NCH):
        pack(ch)

    def gcopies(ch, st):
        yn, yp, yo = (dev(x, up(y, k), c, z) for k in (1, -1, 2))
        zn, zp, zo = (dev(x, y, c, up(z, k)) for k in (1, -1, 2))
        ym, yq, zm, zq = up(y, -1), up(y, 1), up(z, -1), up(z, 1)
        lo, lo1, lo2 = pl.ds(0, 64), pl.ds(0, 32), pl.ds(32, 32)
        hi, hi1, hi2 = pl.ds(64, 64), pl.ds(64, 32), pl.ds(96, 32)
        al = pl.ds(0, N)
        if st == 0:
            mine, yours = (y, z, lo), (y, z, hi)
            parts = [(mine, yn), (mine, yp), (yours, zn), (yours, zp), (mine, yo), (yours, zo)]
        elif st == 1:
            parts = [((al, z, lo), zn), ((al, z, lo), zp), ((y, al, hi), yn), ((y, al, hi), yp)]
        else:
            parts = [((al, zm, lo1), zn), ((al, zq, lo2), zp), ((ym, al, hi1), yn), ((yq, al, hi2), yp)]
        return [
            remote(G.at[(ch,) + p], G.at[(ch,) + p], ggs.at[ch, st * 6 + n], ggr.at[ch, st * 6 + n], to)
            for n, (p, to) in enumerate(parts)
        ]

    def gstep(ch, st):
        if st == 0:
            dsh[ch].wait_recv()
            G[ch, y, z] = keep[ch] + sin_[ch]
        else:
            for d in gcopies(ch, st - 1):
                d.wait_recv()
        if st < 3:
            for d in gcopies(ch, st):
                d.start()

    for d in dg:
        d.wait_recv()
    for k in range(N):
        remote(raw.at[own], raw.at[16 + k], sxs.at[k], sxr.at[k], group[0]).wait_recv()

    slot_l = lax.broadcasted_iota(I32, (PTS, 256), 1).astype(F32)
    pos = lax.broadcasted_iota(I32, (PTS, 256), 0).astype(F32)

    def terms(k):
        a1, a2, a3 = split3(raw[k])
        return jnp.concatenate([a1, a1, a2, a1, a2, a3, jnp.zeros((80, 256), F32)], 0).astype(BF16)

    def chosen(dev_q, first):
        off, num = wide(shv[pl.ds(dev_q, 1), :]), wide(cnv[pl.ds(dev_q, 1), :])
        return jnp.where((pos + first - slot_l == off) & (slot_l < num), 1.0, 0.0).astype(BF16)

    def placed(yy, zz):
        qb = ((x * N + yy) * 2 + c) * N + zz
        ahead = jnp.where(zz == 0, 16 + yy, yy * N + zz - 1)
        dims = (((1,), (1,)), ((), ()))
        kept = lax.dot_general(chosen(qb, 0.0), terms(yy * N + zz), dims, preferred_element_type=F32)
        came = lax.dot_general(
            chosen(lax.rem(qb + 127, 128), 128.0), terms(ahead), dims, preferred_element_type=F32
        )
        return (kept + came).astype(BF16)

    @pl.loop(0, 16)
    def _(b):
        yy, zz = b // N, lax.rem(b, N)
        X[pl.ds(pl.multiple_of(b * PTS, PTS), PTS), :] = placed(yy, zz)

    @pl.loop(0, 16)
    def _(it):
        t, i = it // 4, lax.rem(it, 4)
        for h in range(2):
            rows = pl.multiple_of(i * 512 + h * 256, 256)
            xm = X[pl.ds(rows, 256), :]
            for j in range(2):
                cols = slice(j * 256, (j + 1) * 256)
                turn = jnp.dot(xm, kmat[t, :, cols], preferred_element_type=F32)
                r = turn - jnp.round(turn)
                r2 = r * r
                s = r * horner(r2, SIN)
                E[t, pl.ds(rows, 256), cols] = (1.0 - s * s).astype(BF16)
                E[t, pl.ds(pl.multiple_of(rows + 2048, 256), 256), cols] = (s * horner(r2, COS)).astype(BF16)
        for k, steps in E_STEPS.items():
            @pl.when(it == k)
            def _():
                for ch, st in steps:
                    gstep(ch, st)

    xn, xp, other = dev(up(x, 1), y, c, z), dev(up(x, -1), y, c, z), dev(x, y, 1 - c, z)

    def core_copy(ch, t):
        m = ch * 4 + t
        return remote(Po.at[m], Cx.at[m], cxs.at[m], cxr.at[m], other)

    def half_copy(ch, n):
        land, to = ((Hp, xn), (Hm, xp))[n]
        k = n * NCH + ch
        return remote(Pm.at[ch * 4, pl.ds(64 * n, 64)], land.at[ch], hs.at[k], hr.at[k], to)

    def full_copy(ch, n):
        land, to = ((Rp, xn), (Rm, xp))[n]
        k = n * NCH + ch
        return remote(Pm.at[ch * 4 + 1 + n], land.at[ch], rs.at[k], rr.at[k], to)

    def core_done(ch, t):
        core_copy(ch, t).wait_recv()
        m = ch * 4 + t
        Pm[m] = Pm[m] + Cx[m]
        if t == 0:
            half_copy(ch, 0).start()
            half_copy(ch, 1).start()

    def forward(ch):
        for n in range(2):
            half_copy(ch, n).wait_recv()
            here = pl.ds(64 * n, 64)
            Pm[ch * 4 + 1 + n, here] = Pm[ch * 4 + 1 + n, here] + (Hp, Hm)[n][ch]
            full_copy(ch, n).start()

    def finish(ch):
        full_copy(ch, 0).wait_recv()
        full_copy(ch, 1).wait_recv()
        res = Pm[ch * 4 + 3] + Rp[ch] + Rm[ch]
        out[pl.ds(pl.multiple_of(ch * HB, HB), HB), :] = res[0:64]
        out[pl.ds(pl.multiple_of(256 + ch * HB, HB), HB), :] = res[64:128]

    def build(ch):
        for b in range(16):
            g = G[ch, b // N, b % N]
            lo, hi = g[0:64].astype(BF16), g[64:128].astype(BF16)
            cols, cols2 = slice(b * PTS, (b + 1) * PTS), slice(2048 + b * PTS, 2048 + (b + 1) * PTS)
            L[0:64, cols] = lo
            L[0:64, cols2] = hi
            L[64:128, cols] = hi
            L[64:128, cols2] = -lo

    def product(ch, t):
        part = jnp.dot(L[...], E[t], preferred_element_type=F32)
        Pm[ch * 4 + t] = part[:, :BLK]
        Po[ch * 4 + t] = part[:, BLK:]
        core_copy(ch, t).start()

    def m_steps(m):
        for ch, st in M_STEPS.get(m, []):
            gstep(ch, st)

    @pl.loop(0, 4 * NCH)
    def _(m):
        ch, t = m // 4, lax.rem(m, 4)

        @pl.when(t == 0)
        def _():
            build(ch)

        product(ch, t)
        for k in range(4):
            @pl.when((t == k) & (m > 1))
            def _():
                core_done(ch - (1 if k < 2 else 0), (k + 2) % 4)
                if k == 2:
                    @pl.when(ch > 0)
                    def _():
                        forward(ch - 1)
        for k in M_STEPS:
            @pl.when(m == k)
            def _():
                m_steps(k)

    core_done(NCH - 1, 2)
    forward(NCH - 1)
    core_done(NCH - 1, 3)
    for ch in range(NCH):
        finish(ch)

    for d in n1 + n2 + dsh + dg:
        d.wait_send()

    @pl.when(z == N - 1)
    def _():
        for k in range(16):
            end_copy(k).wait_send()

    for ch in range(NCH):
        for st in range(3):
            for d in gcopies(ch, st):
                d.wait_send()
        for n in range(2):
            half_copy(ch, n).wait_send()
            full_copy(ch, n).wait_send()
        for t in range(4):
            core_copy(ch, t).wait_send()


def local(densities, weights, coords, counts, wave):
    vm, hbm = pl.BlockSpec(memory_space=pltpu.VMEM), pl.BlockSpec(memory_space=pl.ANY)
    dma = pltpu.SemaphoreType.DMA
    out = pl.pallas_call(
        kernel,
        out_shape=jax.ShapeDtypeStruct((512, BLK), F32),
        in_specs=[hbm, hbm, hbm, pl.BlockSpec(memory_space=pltpu.SMEM), hbm],
        out_specs=vm,
        scratch_shapes=[
            pltpu.VMEM((512, 256), F32),
            pltpu.VMEM((1, 256), F32),
            pltpu.VMEM((3, 256), F32),
            pltpu.VMEM((3, 1, 8192), F32),
            pltpu.VMEM((NCH, 128, 256), BF16),
            pltpu.VMEM((8, 8, 128), I32),
            pltpu.VMEM((16, 8, 128), I32),
            pltpu.VMEM((20, 8, 256), F32),
            pltpu.VMEM((128, 128), F32),
            pltpu.VMEM((128, 128), F32),
            pltpu.VMEM((8, NDIR), F32),
            pltpu.VMEM((4, 128, 512), BF16),
            pltpu.VMEM((2048, 128), BF16),
            pltpu.VMEM((NCH, 128, 128), F32),
            pltpu.VMEM((NCH, 128, 128), F32),
            pltpu.VMEM((NCH, 128, 128), F32),
            pltpu.VMEM((NCH, N, N, 128, 128), F32),
            pltpu.VMEM((4, 4096, 512), BF16),
            pltpu.VMEM((128, 4096), BF16),
            pltpu.VMEM((16, 128, BLK), F32),
            pltpu.VMEM((16, 128, BLK), F32),
            pltpu.VMEM((16, 128, BLK), F32),
            pltpu.VMEM((NCH, 64, BLK), F32),
            pltpu.VMEM((NCH, 64, BLK), F32),
            pltpu.VMEM((NCH, 128, BLK), F32),
            pltpu.VMEM((NCH, 128, BLK), F32),
            dma((4,)),
            dma((7,)), dma((7,)),
            dma((15,)), dma((15,)),
            dma((15,)), dma((15,)),
            dma((16,)), dma((N,)),
            dma((NCH,)), dma((NCH,)),
            dma((NCH, 18)), dma((NCH, 18)),
            dma((16,)), dma((16,)),
            dma((2 * NCH,)), dma((2 * NCH,)),
            dma((2 * NCH,)), dma((2 * NCH,)),
        ],
        compiler_params=pltpu.CompilerParams(
            collective_id=0, has_side_effects=True, vmem_limit_bytes=56 * 2**20
        ),
        cost_estimate=pl.CostEstimate(flops=8_600_000_000, bytes_accessed=2_000_000, transcendentals=0),
        name="far_field",
    )(densities, weights.reshape(1, -1), coords, counts, wave)
    return out[:, None, :]


def solution(mesh):
    placed = (
        P(None, ("surf", "dir")),
        P(("surf", "dir")),
        P(None, ("surf", "dir")),
        P(("surf", "dir")),
        P(None, "dir", None),
    )
    return jax.shard_map(
        local, mesh=mesh, in_specs=placed, out_specs=P(None, "dir", "surf"), check_vma=False
    )
```

```python
import functools
import math

import numpy as np

import jax
import jax.numpy as jnp
from jax import lax
from jax.experimental import pallas as pl
from jax.experimental.pallas import tpu as pltpu
from jax.sharding import PartitionSpec as P

MESH = pl.DeviceIdType.MESH
F32, BF16, I32 = jnp.float32, jnp.bfloat16, jnp.int32
N = 4
PTS = 128
NCH = 4
HB = 64
NDIR = 2048
BLK = 256


def _fit(f, terms, odd):
    x = np.cos(np.linspace(0, np.pi / 2, 2001)) * 0.5
    a = np.stack([x ** (2 * k + odd) for k in range(terms)], 1)
    w = np.ones_like(x)
    for _ in range(60):
        c = np.linalg.lstsq(a * w[:, None], f(x) * w, rcond=None)[0]
        e = np.abs(a @ c - f(x))
        w = w * np.sqrt(e / e.max() + 0.02)
        w = w / w.max()
    return [float(np.float32(v)) for v in c * math.sqrt(2.0)]


SIN = _fit(lambda r: np.sin(np.pi * r), 3, 1)
COS = _fit(lambda r: np.cos(np.pi * r), 4, 0)


def horner(q, c):
    acc = c[-1] * q + c[-2]
    for k in c[-3::-1]:
        acc = acc * q + k
    return acc


def split3(v):
    a = v.astype(BF16).astype(F32)
    b = (v - a).astype(BF16).astype(F32)
    return a, b, (v - a) - b


E_STEPS = {1: [(0, 0)], 2: [(1, 0)], 3: [(2, 0)], 4: [(3, 0)], 5: [(0, 1)], 7: [(1, 1)], 10: [(0, 2)], 11: [(2, 1)], 13: [(1, 2)], 14: [(3, 1)], 15: [(0, 3)]}
M_STEPS = {2: [(2, 2)], 3: [(1, 3)], 6: [(3, 2)], 7: [(2, 3)], 11: [(3, 3)]}


def kernel(
    dens_h, wts_h, coords_h, counts, wave_h, out,
    dens, wts, coords, wave, W, cnt1, cnt2, raw, shv, cnv, kf, kmat, X, keep, sout, sin_, G, E, L, Pm, Po, Cx,
    Hp, Hm, Rp, Rm,
    ins, s1s, s1r, s2s, s2r, sgs, sgr, sxs, sxr, shs, shr, ggs, ggr, cxs, cxr, hs, hr, rs, rr,
):
    surf, z = lax.axis_index("surf"), lax.axis_index("dir")
    x, y, c = surf // 8, (surf // 2) % N, surf % 2
    q = surf * N + z

    def dev(xx, yy, cc, zz):
        return ((xx * N + yy) * 2 + cc, zz)

    def up(v, k):
        return lax.rem(v + (k + N), N)

    def remote(src, dst, ss, rs_, to):
        return pltpu.make_async_remote_copy(
            src_ref=src, dst_ref=dst, send_sem=ss, recv_sem=rs_, device_id=to, device_id_type=MESH
        )

    me8 = c * N + z
    peers8 = []
    for k in range(1, 8):
        o = lax.rem(me8 + k, 8)
        peers8.append(dev(x, y, o // N, lax.rem(o, N)))
    peers16 = [dev(up(x, i), up(y, j), c, z) for i in range(N) for j in range(N) if i or j]
    peersyz = [(i, j) for i in range(N) for j in range(N) if i or j]
    qn = lax.rem(q + 1, 128)
    nxt = (qn // N, lax.rem(qn, N))
    run = lax.rem(surf + 1, 32)
    runx, runy, runc = run // 8, (run // 2) % N, run % 2
    group = [dev(runx, i, runc, j) for i in range(N) for j in range(N)]

    barrier = pltpu.get_barrier_semaphore()
    greet = peers8 + peers16
    for to in greet:
        pl.semaphore_signal(barrier, inc=1, device_id=to, device_id_type=MESH)
    fetch = [
        pltpu.make_async_copy(a, b, ins.at[k])
        for k, (a, b) in enumerate(((dens_h, dens), (wts_h, wts), (coords_h, coords), (wave_h, wave)))
    ]
    for d in fetch:
        d.start()
    cnt = counts[0]
    own = y * N + z
    raw[own] = jnp.zeros((8, 256), F32)
    cnt1[me8] = jnp.full((8, 128), cnt, I32)
    pl.semaphore_wait(barrier, len(greet))

    n1 = [
        remote(cnt1.at[me8], cnt1.at[me8], s1s.at[k], s1r.at[k], peers8[k]) for k in range(7)
    ]
    for d in n1:
        d.start()

    for d in fetch:
        d.wait()
    scale = 1.0 / math.sqrt(PTS * 128)
    w = wts[...]
    for ch in range(NCH):
        W[ch, 0:HB] = ((w * dens[ch * HB : (ch + 1) * HB, :]) * scale).astype(BF16)
        W[ch, HB:] = ((w * dens[256 + ch * HB : 256 + (ch + 1) * HB, :]) * scale).astype(BF16)
    for d in n1:
        d.wait_recv()
    eight = jnp.zeros((8, 128), I32)
    line = lax.broadcasted_iota(I32, (8, 128), 0)
    for k in range(8):
        eight = jnp.where(line == k, cnt1[k], eight)
    me16 = x * N + y
    cnt2[me16] = eight
    n2 = [
        remote(cnt2.at[me16], cnt2.at[me16], s2s.at[k], s2r.at[k], peers16[k]) for k in range(15)
    ]
    for d in n2:
        d.start()

    raw[own, 0:3] = coords[...]
    dg = [
        remote(raw.at[own], raw.at[own], sgs.at[k], sgr.at[k], dev(x, up(y, i), c, up(z, j)))
        for k, (i, j) in enumerate(peersyz)
    ]
    for d in dg:
        d.start()

    def end_copy(k):
        return remote(raw.at[own], raw.at[16 + runy], sxs.at[k], sxr.at[runy], group[k])

    @pl.when(z == N - 1)
    def _():
        for k in range(16):
            end_copy(k).start()

    kf[...] = jnp.zeros_like(kf)
    for t, dx in enumerate((2, 1, 3, 0)):
        for h in range(2):
            cc = c if h == 0 else 1 - c
            at = pl.multiple_of((up(x, dx) * 8 + y * 2 + cc) * BLK, BLK)
            for k in range(3):
                kf[k : k + 1, t * 512 + h * BLK : t * 512 + (h + 1) * BLK] = (
                    wave[k, :, pl.ds(at, BLK)] * (1.0 / (2.0 * math.pi))
                )
    k1, k2, k3 = split3(kf[...])
    turns = jnp.concatenate([k1, k2, k1, k3, k2, k1, jnp.zeros((80, NDIR), F32)], 0).astype(BF16)
    for t in range(4):
        kmat[t] = turns[:, t * 512 : (t + 1) * 512]

    for d in n2:
        d.wait_recv()
    nums = cnt2[...].reshape(128, 128).astype(F32)
    at_row = lax.broadcasted_iota(I32, (128, 128), 0)
    at_col = lax.broadcasted_iota(I32, (128, 128), 1)
    lower = jnp.where(at_col < at_row, 1.0, 0.0).astype(BF16)
    cnv[...] = nums
    shv[...] = jnp.dot(lower, nums.astype(BF16), preferred_element_type=F32) - (at_row * PTS).astype(F32)

    def wide(row):
        return jnp.concatenate([row, row], 1)

    slot = lax.broadcasted_iota(I32, (256, 256), 0).astype(F32)
    col = lax.broadcasted_iota(I32, (256, 256), 1).astype(F32)
    myshift, mycnt = wide(shv[pl.ds(q, 1), :]), wide(cnv[pl.ds(q, 1), :])
    pick = jnp.where((col - slot == myshift) & (slot < mycnt), 1.0, 0.0).astype(BF16)

    dsh = [remote(sout.at[ch], sin_.at[ch], shs.at[ch], shr.at[ch], nxt) for ch in range(NCH)]

    def pack(ch):
        moved = jnp.dot(W[ch], pick, preferred_element_type=F32)
        keep[ch] = moved[:, :128]
        sout[ch] = moved[:, 128:]
        dsh[ch].start()

    for ch in range(NCH):
        pack(ch)

    def gcopies(ch, st):
        yn, yp, yo = (dev(x, up(y, k), c, z) for k in (1, -1, 2))
        zn, zp, zo = (dev(x, y, c, up(z, k)) for k in (1, -1, 2))
        ym, yq, zm, zq = up(y, -1), up(y, 1), up(z, -1), up(z, 1)
        lo, lo1, lo2 = pl.ds(0, 64), pl.ds(0, 32), pl.ds(32, 32)
        hi, hi1, hi2 = pl.ds(64, 64), pl.ds(64, 32), pl.ds(96, 32)
        al = pl.ds(0, N)
        if st == 0:
            mine, yours = (y, z, lo), (y, z, hi)
            parts = [(mine, yn), (mine, yp), (yours, zn), (yours, zp), (mine, yo), (yours, zo)]
        elif st == 1:
            parts = [((al, z, lo), zn), ((al, z, lo), zp), ((y, al, hi), yn), ((y, al, hi), yp)]
        else:
            parts = [((al, zm, lo1), zn), ((al, zq, lo2), zp), ((ym, al, hi1), yn), ((yq, al, hi2), yp)]
        return [
            remote(G.at[(ch,) + p], G.at[(ch,) + p], ggs.at[ch, st * 6 + n], ggr.at[ch, st * 6 + n], to)
            for n, (p, to) in enumerate(parts)
        ]

    def gstep(ch, st):
        if st == 0:
            dsh[ch].wait_recv()
            G[ch, y, z] = keep[ch] + sin_[ch]
        else:
            for d in gcopies(ch, st - 1):
                d.wait_recv()
        if st < 3:
            for d in gcopies(ch, st):
                d.start()

    for d in dg:
        d.wait_recv()
    for k in range(N):
        remote(raw.at[own], raw.at[16 + k], sxs.at[k], sxr.at[k], group[0]).wait_recv()

    slot_l = lax.broadcasted_iota(I32, (PTS, 256), 1).astype(F32)
    pos = lax.broadcasted_iota(I32, (PTS, 256), 0).astype(F32)

    def terms(k):
        a1, a2, a3 = split3(raw[k])
        return jnp.concatenate([a1, a1, a2, a1, a2, a3, jnp.zeros((80, 256), F32)], 0).astype(BF16)

    def chosen(dev_q, first):
        off, num = wide(shv[pl.ds(dev_q, 1), :]), wide(cnv[pl.ds(dev_q, 1), :])
        return jnp.where((pos + first - slot_l == off) & (slot_l < num), 1.0, 0.0).astype(BF16)

    def placed(yy, zz):
        qb = ((x * N + yy) * 2 + c) * N + zz
        ahead = jnp.where(zz == 0, 16 + yy, yy * N + zz - 1)
        dims = (((1,), (1,)), ((), ()))
        kept = lax.dot_general(chosen(qb, 0.0), terms(yy * N + zz), dims, preferred_element_type=F32)
        came = lax.dot_general(
            chosen(lax.rem(qb + 127, 128), 128.0), terms(ahead), dims, preferred_element_type=F32
        )
        return (kept + came).astype(BF16)

    @pl.loop(0, 16)
    def _(b):
        yy, zz = b // N, lax.rem(b, N)
        X[pl.ds(pl.multiple_of(b * PTS, PTS), PTS), :] = placed(yy, zz)

    @pl.loop(0, 16)
    def _(it):
        t, i = it // 4, lax.rem(it, 4)
        for h in range(2):
            rows = pl.multiple_of(i * 512 + h * 256, 256)
            xm = X[pl.ds(rows, 256), :]
            for j in range(2):
                cols = slice(j * 256, (j + 1) * 256)
                turn = jnp.dot(xm, kmat[t, :, cols], preferred_element_type=F32)
                r = turn - jnp.round(turn)
                r2 = r * r
                s = r * horner(r2, SIN)
                E[t, pl.ds(rows, 256), cols] = (1.0 - s * s).astype(BF16)
                E[t, pl.ds(pl.multiple_of(rows + 2048, 256), 256), cols] = (s * horner(r2, COS)).astype(BF16)
        for k, steps in E_STEPS.items():
            @pl.when(it == k)
            def _():
                for ch, st in steps:
                    gstep(ch, st)

    xn, xp, other = dev(up(x, 1), y, c, z), dev(up(x, -1), y, c, z), dev(x, y, 1 - c, z)

    def core_copy(ch, t):
        m = ch * 4 + t
        return remote(Po.at[m], Cx.at[m], cxs.at[m], cxr.at[m], other)

    def half_copy(ch, n):
        land, to = ((Hp, xn), (Hm, xp))[n]
        k = n * NCH + ch
        return remote(Pm.at[ch * 4, pl.ds(64 * n, 64)], land.at[ch], hs.at[k], hr.at[k], to)

    def full_copy(ch, n):
        land, to = ((Rp, xn), (Rm, xp))[n]
        k = n * NCH + ch
        return remote(Pm.at[ch * 4 + 1 + n], land.at[ch], rs.at[k], rr.at[k], to)

    def core_done(ch, t):
        core_copy(ch, t).wait_recv()
        m = ch * 4 + t
        Pm[m] = Pm[m] + Cx[m]
        if t == 0:
            half_copy(ch, 0).start()
            half_copy(ch, 1).start()

    def forward(ch):
        for n in range(2):
            half_copy(ch, n).wait_recv()
            here = pl.ds(64 * n, 64)
            Pm[ch * 4 + 1 + n, here] = Pm[ch * 4 + 1 + n, here] + (Hp, Hm)[n][ch]
            full_copy(ch, n).start()

    def finish(ch):
        full_copy(ch, 0).wait_recv()
        full_copy(ch, 1).wait_recv()
        res = Pm[ch * 4 + 3] + Rp[ch] + Rm[ch]
        out[pl.ds(pl.multiple_of(ch * HB, HB), HB), :] = res[0:64]
        out[pl.ds(pl.multiple_of(256 + ch * HB, HB), HB), :] = res[64:128]

    def build(ch):
        for b in range(16):
            g = G[ch, b // N, b % N]
            lo, hi = g[0:64].astype(BF16), g[64:128].astype(BF16)
            cols, cols2 = slice(b * PTS, (b + 1) * PTS), slice(2048 + b * PTS, 2048 + (b + 1) * PTS)
            L[0:64, cols] = lo
            L[0:64, cols2] = hi
            L[64:128, cols] = hi
            L[64:128, cols2] = -lo

    def product(ch, t):
        part = jnp.dot(L[...], E[t], preferred_element_type=F32)
        Pm[ch * 4 + t] = part[:, :BLK]
        Po[ch * 4 + t] = part[:, BLK:]
        core_copy(ch, t).start()

    def m_steps(m):
        for ch, st in M_STEPS.get(m, []):
            gstep(ch, st)

    @pl.loop(0, 4 * NCH)
    def _(m):
        ch, t = m // 4, lax.rem(m, 4)

        @pl.when(t == 0)
        def _():
            build(ch)

        product(ch, t)
        for k in range(4):
            @pl.when((t == k) & (m > 1))
            def _():
                core_done(ch - (1 if k < 2 else 0), (k + 2) % 4)
                if k == 2:
                    @pl.when(ch > 0)
                    def _():
                        forward(ch - 1)
        for k in M_STEPS:
            @pl.when(m == k)
            def _():
                m_steps(k)

    core_done(NCH - 1, 2)
    forward(NCH - 1)
    core_done(NCH - 1, 3)
    for ch in range(NCH):
        finish(ch)

    for d in n1 + n2 + dsh + dg:
        d.wait_send()

    @pl.when(z == N - 1)
    def _():
        for k in range(16):
            end_copy(k).wait_send()

    for ch in range(NCH):
        for st in range(3):
            for d in gcopies(ch, st):
                d.wait_send()
        for n in range(2):
            half_copy(ch, n).wait_send()
            full_copy(ch, n).wait_send()
        for t in range(4):
            core_copy(ch, t).wait_send()


def local(densities, weights, coords, counts, wave):
    vm, hbm = pl.BlockSpec(memory_space=pltpu.VMEM), pl.BlockSpec(memory_space=pl.ANY)
    dma = pltpu.SemaphoreType.DMA
    out = pl.pallas_call(
        kernel,
        out_shape=jax.ShapeDtypeStruct((512, BLK), F32),
        in_specs=[hbm, hbm, hbm, pl.BlockSpec(memory_space=pltpu.SMEM), hbm],
        out_specs=vm,
        scratch_shapes=[
            pltpu.VMEM((512, 256), F32),
            pltpu.VMEM((1, 256), F32),
            pltpu.VMEM((3, 256), F32),
            pltpu.VMEM((3, 1, 8192), F32),
            pltpu.VMEM((NCH, 128, 256), BF16),
            pltpu.VMEM((8, 8, 128), I32),
            pltpu.VMEM((16, 8, 128), I32),
            pltpu.VMEM((20, 8, 256), F32),
            pltpu.VMEM((128, 128), F32),
            pltpu.VMEM((128, 128), F32),
            pltpu.VMEM((8, NDIR), F32),
            pltpu.VMEM((4, 128, 512), BF16),
            pltpu.VMEM((2048, 128), BF16),
            pltpu.VMEM((NCH, 128, 128), F32),
            pltpu.VMEM((NCH, 128, 128), F32),
            pltpu.VMEM((NCH, 128, 128), F32),
            pltpu.VMEM((NCH, N, N, 128, 128), F32),
            pltpu.VMEM((4, 4096, 512), BF16),
            pltpu.VMEM((128, 4096), BF16),
            pltpu.VMEM((16, 128, BLK), F32),
            pltpu.VMEM((16, 128, BLK), F32),
            pltpu.VMEM((16, 128, BLK), F32),
            pltpu.VMEM((NCH, 64, BLK), F32),
            pltpu.VMEM((NCH, 64, BLK), F32),
            pltpu.VMEM((NCH, 128, BLK), F32),
            pltpu.VMEM((NCH, 128, BLK), F32),
            dma((4,)),
            dma((7,)), dma((7,)),
            dma((15,)), dma((15,)),
            dma((15,)), dma((15,)),
            dma((16,)), dma((N,)),
            dma((NCH,)), dma((NCH,)),
            dma((NCH, 18)), dma((NCH, 18)),
            dma((16,)), dma((16,)),
            dma((2 * NCH,)), dma((2 * NCH,)),
            dma((2 * NCH,)), dma((2 * NCH,)),
        ],
        compiler_params=pltpu.CompilerParams(
            collective_id=0, has_side_effects=True, vmem_limit_bytes=56 * 2**20
        ),
        cost_estimate=pl.CostEstimate(flops=8_600_000_000, bytes_accessed=2_000_000, transcendentals=0),
        name="far_field",
    )(densities, weights.reshape(1, -1), coords, counts, wave)
    return out[:, None, :]


def solution(mesh):
    placed = (
        P(None, ("surf", "dir")),
        P(("surf", "dir")),
        P(None, ("surf", "dir")),
        P(("surf", "dir")),
        P(None, "dir", None),
    )
    return jax.shard_map(
        local, mesh=mesh, in_specs=placed, out_specs=P(None, "dir", "surf"), check_vma=False
    )
```
